32 devices in a mesh: row: 8 (over z, y), col: 4 (over x, core).
Axes of the slice: x: 2, y: 2, z: 4, core: 2. Of those that a mesh axis runs over, the one named last changes fastest.
Arguments:
- right_side: float32 [4, 64, 6144], P(None, 'row'), may hold values from -6 to 6
- factor: bfloat16 [4, 64, 128, 4096], P(None, 'row', 'col'), may hold values from -0.0625 to 0.0625
- diagonal_block_inverse: bfloat16 [4, 64, 4096], P(None, 'row'), may hold values from -0.5 to 0.5
- pattern: int32 [4, 64, 128], P(None, 'row', 'col'), may hold values from -1 to 191, as said below
Outputs:
- solution: bfloat16 [4, 64, 6144], P(None, 'row')
The draws below stay inside these ranges and needn't reach their ends.
Inputs may be any that keep to these rules, and one draw needn't show every extreme that they name: `pattern`: level 0 is all -1; at level l an entry is -1 or names a supernode of an earlier level, below l * 64.
All inputs are finite; a program needn't handle non-finite values.
Results may differ from the reference program's by a relative error of at most 0.0055.
Values may be sent and summed in bfloat16 or wider, within the bound.
A program may use at most 128 MiB of HBM per device.

```python
import jax
import jax.numpy as jnp
from jax import lax

B = 64
R = 96
LEVELS = 4
SN_LEV = 64
COLUMN_BLOCKS = 128


def draw_pattern(key, part):
    first = jax.random.fold_in(key, 11)
    second = jax.random.fold_in(key, 23)
    levels = jnp.arange(LEVELS, dtype=jnp.int32)[:, None, None]
    upper = jnp.maximum(levels * SN_LEV, 1)
    shape = (LEVELS, SN_LEV, COLUMN_BLOCKS)
    sources = jax.random.randint(first, shape, 0, upper, dtype=jnp.int32)
    active = jax.random.randint(second, shape, 0, 4, dtype=jnp.int32) > 0
    pattern = jnp.where(active & (levels > 0), sources, -1)
    return pattern.at[LEVELS - 1, 0, 0].set((LEVELS - 1) * SN_LEV - 1)


def steps_of(key, extent, shards, low, high):
    level = 1.0
    for position, parts in shards:
        draws = jax.random.uniform(jax.random.fold_in(jax.random.fold_in(key, 6), position), (parts,), jnp.float32, low / len(shards), high / len(shards))
        level = level * jnp.repeat(jnp.exp(draws), extent[position] // parts).reshape((-1,) + (1,) * (len(extent) - 1 - position))
    return level


def centred(stream_key, extent, spread, bound, split=(), kind=jnp.bfloat16):
    level = steps_of(stream_key, extent, split, -0.22, 0.18) if split else 1.0
    result = jax.random.normal(stream_key, extent, jnp.float32) * spread * level
    return jnp.minimum(jnp.maximum(result, -bound), bound).astype(kind)


def setup_inputs(seed: int = 0) -> dict:
    keys = jax.random.split(jax.random.key(seed), 5)
    return {
        "right_side": centred(keys[0], (LEVELS, SN_LEV, B * R), 1.0, 6.0, ((1, 8),), jnp.float32),
        "factor": centred(keys[1], (LEVELS, SN_LEV, COLUMN_BLOCKS, B * B), (B * COLUMN_BLOCKS) ** -0.5, 0.0625, ((1, 8), (2, 4))),
        "diagonal_block_inverse": centred(keys[2], (LEVELS, SN_LEV, B * B), (2 * B) ** -0.5, 0.5, ((1, 8),)),
        "pattern": draw_pattern(jax.random.fold_in(keys[4], 71), 0),
    }


def reference(right_side, factor, diagonal_block_inverse, pattern):
    panel_blocks = jnp.zeros((LEVELS * SN_LEV, B * R), jnp.bfloat16)
    for level in range(LEVELS):
        sources = pattern[level]
        active = sources >= 0
        clipped = jnp.maximum(sources, 0).astype(jnp.int32)

        def row_product(operands):
            ids, mask, blocks = operands
            picked = jnp.take(panel_blocks, ids, axis=0)
            picked = jnp.where(mask[:, None], picked, jnp.zeros_like(picked))
            picked = picked.reshape(COLUMN_BLOCKS, B, R).astype(jnp.float32)
            mats = blocks.reshape(COLUMN_BLOCKS, B, B).astype(jnp.float32)
            return jnp.einsum("kab,kbr->ar", mats, picked)

        summed_products = lax.map(row_product, (clipped, active, factor[level]))
        reduced_rows = (right_side[level].reshape(SN_LEV, B, R) - summed_products).astype(jnp.bfloat16)
        inverse_block = diagonal_block_inverse[level].reshape(SN_LEV, B, B).astype(jnp.float32)
        solved_rows = jnp.einsum("xuc,xcg->xug", inverse_block, reduced_rows.astype(jnp.float32)).astype(jnp.bfloat16)
        panel_blocks = panel_blocks.at[level * SN_LEV:(level + 1) * SN_LEV].set(solved_rows.reshape(SN_LEV, B * R))
    return panel_blocks.reshape(LEVELS, SN_LEV, B * R)
```

```python
import functools

import jax
import jax.numpy as jnp
from jax import lax
from jax.experimental import pallas as pl
from jax.experimental.pallas import tpu as pltpu
from jax.sharding import PartitionSpec as P

B = 64
R = 96
LANES = 128
PACK = 48
MESH = pl.DeviceIdType.MESH


def pack(value):
    tail = value[PACK:, :R]
    third = B - PACK
    side = jnp.concatenate([tail[:, 32 * j : 32 * j + 32] for j in range(PACK // third)], axis=0)
    return jnp.concatenate([value[:PACK, :R], side], axis=1)


def unpack_tail(packed):
    third = B - PACK
    parts = [packed[third * j : third * (j + 1), R:] for j in range(PACK // third)]
    return jnp.concatenate(parts, axis=1)


def kernel(
    sizes, pattern_ref, right_ref, inverse_ref, factor_ref, out_ref,
    raw, ready, turn, panels, psend, mine, precv, land, last,
    fsem, red_send, red_recv, z_send, y_send, x_send, c_send,
    z_recv, y_recv, x_recv, c_recv, l_send, l_recv,
):
    levels, sn_dev, slots, Z, Y, X = sizes
    col_count = 2 * X
    row_count = Z * Y
    own = sn_dev // col_count
    sn_lev = sn_dev * row_count
    empty = (levels - 1) * sn_lev
    row = lax.axis_index("row")
    col = lax.axis_index("col")
    z, y = row // Y, row % Y
    x, core = col // 2, col % 2

    loads = [
        pltpu.make_async_copy(factor_ref.at[l + 1], raw.at[l], fsem.at[l]) for l in range(levels - 1)
    ]
    for load in loads:
        load.start()

    zs = [(z + d) % Z for d in range(1, Z)]
    ys = [(y + d) % Y for d in range(1, Y)]
    xs = [(x + d) % X for d in range(1, X)]
    cols = [(col + d) % col_count for d in range(1, col_count)]

    def at(r, c):
        return {"row": r, "col": c}

    barrier = pltpu.get_barrier_semaphore()
    for t in zs:
        pl.semaphore_signal(barrier, inc=1, device_id=at(t * Y + y, col), device_id_type=MESH)
    for t in ys:
        pl.semaphore_signal(barrier, inc=1, device_id=at(z * Y + t, col), device_id_type=MESH)
    for t in cols:
        pl.semaphore_signal(barrier, inc=1, device_id=at(row, t), device_id_type=MESH)

    def remote(src, dst, send, recv, device):
        return pltpu.make_async_remote_copy(
            src_ref=src, dst_ref=dst, send_sem=send, recv_sem=recv,
            device_id=device, device_id_type=MESH,
        )

    def solve(level, summed):
        for u in range(own):
            value = right_ref[level, u]
            if summed is not None:
                value = value - summed[u]
            solved = jnp.dot(
                inverse_ref[level, u], value.astype(jnp.bfloat16), preferred_element_type=jnp.float32
            )
            mine[level, u * PACK : (u + 1) * PACK, :] = pack(solved).astype(jnp.bfloat16)

    def prepare(level):
        loads[level - 1].wait()
        low = lax.broadcasted_iota(jnp.int32, (B // 2, LANES), 1) < B

        def body(i, carry):
            for a in range(B // 2):
                turn[:, a, :] = raw[level - 1, i, :, a * LANES : (a + 1) * LANES].astype(jnp.float32)
            for q in range(slots // 2):
                first, second = turn[2 * q], turn[2 * q + 1]
                lanes = slice(q * LANES, (q + 1) * LANES)
                ready[level - 1, i, : B // 2, lanes] = jnp.where(
                    low, first, pltpu.roll(second, B, 1)
                ).astype(jnp.bfloat16)
                ready[level - 1, i, B // 2 :, lanes] = jnp.where(
                    low, pltpu.roll(first, B, 1), second
                ).astype(jnp.bfloat16)
            return carry

        lax.fori_loop(0, sn_dev, body, 0)

    def products(level):
        def body(n, carry):
            target = (col + 1 + n // own) % col_count
            u = n % own
            i = target * own + u
            total = jnp.zeros((B, LANES), jnp.float32)
            for q in range(slots // 4):
                picked = []
                for k in range(4 * q, 4 * q + 4):
                    source = pattern_ref[level, i, k]
                    picked.append(panels[jnp.where(source < 0, empty, source)])
                total += jnp.dot(
                    ready[level - 1, i, :, 4 * B * q : 4 * B * (q + 1)],
                    jnp.concatenate(picked, axis=0),
                    preferred_element_type=jnp.float32,
                )
            psend[target, pl.ds(pl.multiple_of(u * PACK, PACK), PACK), :] = pack(total)
            return carry

        copies = []
        for d in range(1, col_count):
            lax.fori_loop((d - 1) * own, d * own, body, 0)
            t = cols[d - 1]
            copy = remote(
                psend.at[t], precv[level - 1].at[col],
                red_send.at[t], red_recv.at[level - 1, col], at(row, t),
            )
            copy.start()
            copies.append(copy)
        lax.fori_loop((col_count - 1) * own, col_count * own, body, 0)
        summed = psend[col]
        for t in cols:
            remote(
                psend.at[t], precv[level - 1].at[t],
                red_send.at[t], red_recv.at[level - 1, t], at(row, t),
            ).wait_recv()
            summed += precv[level - 1][t]
        for copy in copies:
            copy.wait_send()
        values = []
        for u in range(own):
            packed = summed[u * PACK : (u + 1) * PACK]
            values.append(jnp.concatenate([packed[:, :R], unpack_tail(packed)], axis=0))
        return values

    def spread(peers, where, region, land_level, send, recv, index):
        copies = []
        for t in peers:
            copy = remote(region(index), region(index), send.at[t], recv.at[index], where(t))
            copy.start()
            copies.append(copy)
        return copies

    def collect(peers, where, region, send, recv):
        for t in peers:
            remote(region(t), region(t), send.at[t], recv.at[t], where(t)).wait_recv()

    def gather(level, beside):
        here = land[level]
        own_copy = pltpu.make_async_copy(mine.at[level], here.at[z, y, x, core], fsem.at[levels - 1])
        own_copy.start()
        own_copy.wait()

        def z_region(t):
            return here.at[t, y, x, core]

        def z_where(t):
            return at(t * Y + y, col)

        def y_where(t):
            return at(z * Y + t, col)

        def x_where(t):
            return at(row, t * 2 + core)

        zc = spread(zs, z_where, z_region, here, z_send, z_recv.at[level], z)
        beside()
        collect(zs, z_where, z_region, z_send, z_recv.at[level])

        def along(y_region, x_region, y_first):
            def do_y():
                cs = spread(ys, y_where, y_region, here, y_send, y_recv.at[level], y)
                collect(ys, y_where, y_region, y_send, y_recv.at[level])
                return cs

            def do_x():
                cs = spread(xs, x_where, x_region, here, x_send, x_recv.at[level], x)
                collect(xs, x_where, x_region, x_send, x_recv.at[level])
                return cs

            cs = do_y() + do_x() if y_first else do_x() + do_y()
            for copy in cs:
                copy.wait_send()

        @pl.when(core == 0)
        def _():
            along(lambda t: here.at[:, t, x, core], lambda t: here.at[:, :, t, core], True)

        @pl.when(core == 1)
        def _():
            along(lambda t: here.at[:, t, :, core], lambda t: here.at[:, y, t, core], False)

        for copy in zc:
            copy.wait_send()
        sibling = remote(
            here.at[:, :, :, core], here.at[:, :, :, core],
            c_send.at[0], c_recv.at[level, core], at(row, x * 2 + 1 - core),
        )
        sibling.start()
        remote(
            here.at[:, :, :, 1 - core], here.at[:, :, :, 1 - core],
            c_send.at[0], c_recv.at[level, 1 - core], at(row, x * 2 + 1 - core),
        ).wait_recv()
        sibling.wait_send()

        def body(n, carry):
            zz = n // (Y * X)
            yy = (n // X) % Y
            xx = n % X
            base = level * sn_lev + n * (2 * own)
            for c in range(2):
                for u in range(own):
                    packed = here[zz, yy, xx, c, u * PACK : (u + 1) * PACK, :]
                    g = base + c * own + u
                    panels[g, :PACK, :] = packed
                    panels[g, PACK:, :R] = unpack_tail(packed)
            return carry

        lax.fori_loop(0, Z * Y * X, body, 0)

    panels[empty] = jnp.zeros((B, LANES), jnp.bfloat16)
    solve(0, None)
    pl.semaphore_wait(barrier, Z - 1 + Y - 1 + col_count - 1)
    for level in range(levels):
        if level > 0:
            solve(level, products(level))
        if level < levels - 1:
            gather(level, functools.partial(prepare, level + 1))
            for i in range(sn_dev):
                out_ref[level, i] = panels[level * sn_lev + row * sn_dev + i, :, :R]

    top = levels - 1
    copies = []
    for t in cols:
        copy = remote(mine.at[top], last.at[col], l_send.at[t], l_recv.at[col], at(row, t))
        copy.start()
        copies.append(copy)
    last[col] = mine[top]
    for t in cols:
        remote(mine.at[top], last.at[t], l_send.at[t], l_recv.at[t], at(row, t)).wait_recv()
    for copy in copies:
        copy.wait_send()
    for c in range(col_count):
        for u in range(own):
            packed = last[c, u * PACK : (u + 1) * PACK, :]
            out_ref[top, c * own + u, :PACK, :] = packed[:, :R]
            out_ref[top, c * own + u, PACK:, :] = unpack_tail(packed)


def per_device(right_side, factor, diagonal_block_inverse, pattern):
    levels, sn_dev, _ = right_side.shape
    slots = factor.shape[2]
    row_count = lax.axis_size("row")
    col_count = lax.axis_size("col")
    Y = 1
    while 8 * Y * Y <= row_count:
        Y *= 2
    Z = row_count // Y
    X = col_count // 2
    own = sn_dev // col_count
    sn_lev = sn_dev * row_count
    first = lax.axis_index("col") * own
    right = lax.dynamic_slice_in_dim(right_side, first, own, 1)
    right = right.reshape(levels, own, B // 2, 2, R).swapaxes(2, 3).reshape(levels, own, B, R)
    inverse = lax.dynamic_slice_in_dim(diagonal_block_inverse, first, own, 1)
    inverse = inverse.reshape(levels, own, B, B // 2, 2).swapaxes(3, 4).reshape(levels, own, B, B)
    dma = pltpu.SemaphoreType.DMA
    rows = own * PACK
    solved = pl.pallas_call(
        functools.partial(kernel, (levels, sn_dev, slots, Z, Y, X)),
        out_shape=jax.ShapeDtypeStruct((levels, sn_dev, B, R), jnp.bfloat16),
        in_specs=[
            pl.BlockSpec(memory_space=pltpu.SMEM),
            pl.BlockSpec(memory_space=pltpu.VMEM),
            pl.BlockSpec(memory_space=pltpu.VMEM),
            pl.BlockSpec(memory_space=pl.ANY),
        ],
        out_specs=pl.BlockSpec(memory_space=pltpu.VMEM),
        scratch_shapes=[
            pltpu.VMEM((levels - 1, sn_dev, slots, B * B), jnp.bfloat16),
            pltpu.VMEM((levels - 1, sn_dev, B, slots * B), jnp.bfloat16),
            pltpu.VMEM((slots, B // 2, LANES), jnp.float32),
            pltpu.VMEM(((levels - 1) * sn_lev + 1, B, LANES), jnp.bfloat16),
            pltpu.VMEM((col_count, rows, LANES), jnp.float32),
            pltpu.VMEM((levels, rows, LANES), jnp.bfloat16),
            [pltpu.VMEM((col_count, rows, LANES), jnp.float32) for _ in range(levels - 1)],
            [pltpu.VMEM((Z, Y, X, 2, rows, LANES), jnp.bfloat16) for _ in range(levels - 1)],
            pltpu.VMEM((col_count, rows, LANES), jnp.bfloat16),
            dma((levels,)),
            dma((col_count,)),
            dma((levels - 1, col_count)),
            dma((Z,)),
            dma((Y,)),
            dma((X,)),
            dma((1,)),
            dma((levels - 1, Z)),
            dma((levels - 1, Y)),
            dma((levels - 1, X)),
            dma((levels - 1, 2)),
            dma((col_count,)),
            dma((col_count,)),
        ],
        compiler_params=pltpu.CompilerParams(
            collective_id=0, has_side_effects=True, vmem_limit_bytes=60 * 1024 * 1024
        ),
    )(pattern, right, inverse, factor)
    return solved.reshape(levels, sn_dev, B * R)


def solution(mesh):
    return jax.shard_map(
        per_device,
        mesh=mesh,
        in_specs=(
            P(None, "row", None),
            P(None, "row", "col", None),
            P(None, "row", None),
            P(None, "row", "col"),
        ),
        out_specs=P(None, "row", None),
        check_vma=False,
    )
```

```python
import functools

import jax
import jax.numpy as jnp
from jax import lax
from jax.experimental import pallas as pl
from jax.experimental.pallas import tpu as pltpu
from jax.sharding import PartitionSpec as P

B = 64
R = 96
LANES = 128
PACK = 48
MESH = pl.DeviceIdType.MESH


def pack(value):
    tail = value[PACK:, :R]
    third = B - PACK
    side = jnp.concatenate([tail[:, 32 * j : 32 * j + 32] for j in range(PACK // third)], axis=0)
    return jnp.concatenate([value[:PACK, :R], side], axis=1)


def unpack_tail(packed):
    third = B - PACK
    parts = [packed[third * j : third * (j + 1), R:] for j in range(PACK // third)]
    return jnp.concatenate(parts, axis=1)


def kernel(
    sizes, pattern_ref, right_ref, inverse_ref, factor_ref, out_ref,
    raw, ready, turn, panels, psend, keep, mine, precv, land, last,
    fsem, red_send, red_recv, z_send, s_send, c_send,
    z_recv, s_recv, c_recv, l_send, l_recv,
):
    levels, sn_dev, slots, Z, A = sizes
    col_count = 2 * A
    row_count = Z * A
    own = sn_dev // col_count
    sn_lev = sn_dev * row_count
    empty = (levels - 1) * sn_lev
    row = lax.axis_index("row")
    col = lax.axis_index("col")
    z, y = row // A, row % A
    x, core = col // 2, col % 2

    def load(level):
        return pltpu.make_async_copy(factor_ref.at[level], raw.at[level - 1], fsem.at[level - 1])

    for level in range(1, levels):
        load(level).start()

    turns = 1 + (z // (Z // 2)) * (Z - 2)
    cols = [(col + d) % col_count for d in range(1, col_count)]

    def plane(d):
        return (z + turns * d) % Z

    def at(r, c):
        return {"row": r, "col": c}

    barrier = pltpu.get_barrier_semaphore()
    for d in range(1, Z):
        pl.semaphore_signal(barrier, inc=1, device_id=at(plane(d) * A + y, col), device_id_type=MESH)
    plane_peers = [
        ((y + d // A) % A, (x + d % A) % A) for d in range(1, A * A)
    ]
    for yt, xt in plane_peers:
        pl.semaphore_signal(barrier, inc=1, device_id=at(z * A + yt, xt * 2 + core), device_id_type=MESH)
    for t in range(A):
        pl.semaphore_signal(barrier, inc=1, device_id=at(row, t * 2 + 1 - core), device_id_type=MESH)

    def remote(src, dst, send, recv, device):
        return pltpu.make_async_remote_copy(
            src_ref=src, dst_ref=dst, send_sem=send, recv_sem=recv,
            device_id=device, device_id_type=MESH,
        )

    def solve(level, summed):
        for u in range(own):
            value = right_ref[level, u]
            if summed is not None:
                value = value - summed[u]
            solved = jnp.dot(
                inverse_ref[level, u], value.astype(jnp.bfloat16), preferred_element_type=jnp.float32
            )
            mine[u * PACK : (u + 1) * PACK, :] = pack(solved).astype(jnp.bfloat16)

    def prepare(level, begin, count):
        low = lax.broadcasted_iota(jnp.int32, (B // 2, LANES), 1) < B

        def body(i, carry):
            for a in range(B // 2):
                turn[:, a, :] = raw[level - 1, i, :, a * LANES : (a + 1) * LANES].astype(jnp.float32)
            for q in range(slots // 2):
                even, odd = turn[2 * q], turn[2 * q + 1]
                lanes = slice(q * LANES, (q + 1) * LANES)
                ready[i, : B // 2, lanes] = jnp.where(low, even, pltpu.roll(odd, B, 1)).astype(jnp.bfloat16)
                ready[i, B // 2 :, lanes] = jnp.where(low, pltpu.roll(even, B, 1), odd).astype(jnp.bfloat16)
            return carry

        lax.fori_loop(begin, begin + count, body, 0)

    def products(level):
        def product(i):
            total = jnp.zeros((B, LANES), jnp.float32)
            for q in range(slots // 4):
                picked = []
                for k in range(4 * q, 4 * q + 4):
                    source = pattern_ref[level, i, k]
                    picked.append(panels[jnp.where(source < 0, empty, source)])
                total += jnp.dot(
                    ready[i, :, 4 * B * q : 4 * B * (q + 1)],
                    jnp.concatenate(picked, axis=0),
                    preferred_element_type=jnp.float32,
                )
            return pack(total)

        def copy(t, source):
            return remote(
                psend.at[t], precv.at[level - 1, source],
                red_send.at[t], red_recv.at[level - 1, source], at(row, t),
            )

        for t in cols:
            def outward(u, carry):
                psend[t, pl.ds(pl.multiple_of(u * PACK, PACK), PACK), :] = product(t * own + u).astype(
                    jnp.bfloat16
                )
                return carry

            lax.fori_loop(0, own, outward, 0)
            copy(t, col).start()

        def inward(u, carry):
            keep[pl.ds(pl.multiple_of(u * PACK, PACK), PACK), :] = product(col * own + u)
            return carry

        lax.fori_loop(0, own, inward, 0)
        summed = keep[...]
        for t in cols:
            copy(t, t).wait_recv()
            summed += precv[level - 1, t].astype(jnp.float32)
        for t in cols:
            copy(t, col).wait_send()
        values = []
        for u in range(own):
            packed = summed[u * PACK : (u + 1) * PACK]
            values.append(jnp.concatenate([packed[:, :R], unpack_tail(packed)], axis=0))
        return values

    def unpack(level, zc, yc, xc, c):
        base = level * sn_lev + (((zc * A + yc) * A + xc) * 2 + c) * own
        for u in range(own):
            packed = land[level, zc, yc, xc, c, u * PACK : (u + 1) * PACK, :]
            panels[base + u, :PACK, :] = packed
            panels[base + u, PACK:, :R] = unpack_tail(packed)

    def gather(level):
        def z_copy(t, source):
            part = land.at[level, source, y, x, core]
            return remote(part, part, z_send.at[t], z_recv.at[level, source], at(t * A + y, col))

        def p_copy(zc, yt, xt, yc, xc):
            part = land.at[level, zc, yc, xc, core]
            return remote(
                part, part, s_send.at[zc, yt, xt], s_recv.at[level, zc, yc, xc],
                at(z * A + yt, xt * 2 + core),
            )

        def c_copy(zc, yc, xc, c):
            part = land.at[level, zc, yc, xc, c]
            return remote(
                part, part, c_send.at[zc, yc, xc], c_recv.at[level, zc, yc, xc],
                at(row, x * 2 + 1 - core),
            )

        def done(zc, yc, xc):
            c_copy(zc, yc, xc, core).start()
            unpack(level, zc, yc, xc, core)

        def chunk(zc):
            for yt, xt in plane_peers:
                p_copy(zc, yt, xt, y, x).start()
            done(zc, y, x)

        def tail(zc):
            for yt, xt in plane_peers:
                p_copy(zc, yt, xt, yt, xt).wait_recv()
                done(zc, yt, xt)

        land[level, z, y, x, core] = mine[...]
        for d in range(1, Z):
            z_copy(plane(d), z).start()
        chunk(z)
        load(level + 1).wait()
        share = sn_dev // Z
        prepare(level + 1, 0, share)

        def body(d, carry):
            zc = plane(d)
            z_copy(zc, zc).wait_recv()
            chunk(zc)
            prepare(level + 1, d * share, share)
            tail(plane(d - 1))
            return carry

        lax.fori_loop(1, Z, body, 0)
        tail(plane(Z - 1))

        def finish(zc, carry):
            for yc in range(A):
                for xc in range(A):
                    c_copy(zc, yc, xc, 1 - core).wait_recv()
                    unpack(level, zc, yc, xc, 1 - core)
            return carry

        lax.fori_loop(0, Z, finish, 0)

        for d in range(1, Z):
            z_copy(plane(d), z).wait_send()

        def settle(zc, carry):
            for yt, xt in plane_peers:
                p_copy(zc, yt, xt, y, x).wait_send()
            for yc in range(A):
                for xc in range(A):
                    c_copy(zc, yc, xc, core).wait_send()
            return carry

        lax.fori_loop(0, Z, settle, 0)

    panels[empty] = jnp.zeros((B, LANES), jnp.bfloat16)
    solve(0, None)
    pl.semaphore_wait(barrier, Z - 1 + A * A - 1 + A)

    def step(level, carry):
        gather(level)
        solve(level + 1, products(level + 1))
        return carry

    lax.fori_loop(0, levels - 1, step, 0)

    top = levels - 1

    def top_copy(t, source):
        return remote(mine, last.at[source], l_send.at[t], l_recv.at[source], at(row, t))

    for t in cols:
        top_copy(t, col).start()
    for level in range(top):
        for i in range(sn_dev):
            out_ref[level, i] = panels[level * sn_lev + row * sn_dev + i, :, :R]
    last[col] = mine[...]
    for t in cols:
        top_copy(t, t).wait_recv()
    for t in cols:
        top_copy(t, col).wait_send()
    for c in range(col_count):
        for u in range(own):
            packed = last[c, u * PACK : (u + 1) * PACK, :]
            out_ref[top, c * own + u, :PACK, :] = packed[:, :R]
            out_ref[top, c * own + u, PACK:, :] = unpack_tail(packed)


def per_device(right_side, factor, diagonal_block_inverse, pattern):
    levels, sn_dev, _ = right_side.shape
    slots = factor.shape[2]
    row_count = lax.axis_size("row")
    col_count = lax.axis_size("col")
    A = col_count // 2
    Z = row_count // A
    own = sn_dev // col_count
    sn_lev = sn_dev * row_count
    first = lax.axis_index("col") * own
    right = lax.dynamic_slice_in_dim(right_side, first, own, 1)
    right = right.reshape(levels, own, B // 2, 2, R).swapaxes(2, 3).reshape(levels, own, B, R)
    inverse = lax.dynamic_slice_in_dim(diagonal_block_inverse, first, own, 1)
    inverse = inverse.reshape(levels, own, B, B // 2, 2).swapaxes(3, 4).reshape(levels, own, B, B)
    dma = pltpu.SemaphoreType.DMA
    rows = own * PACK
    solved = pl.pallas_call(
        functools.partial(kernel, (levels, sn_dev, slots, Z, A)),
        out_shape=jax.ShapeDtypeStruct((levels, sn_dev, B, R), jnp.bfloat16),
        in_specs=[
            pl.BlockSpec(memory_space=pltpu.SMEM),
            pl.BlockSpec(memory_space=pltpu.VMEM),
            pl.BlockSpec(memory_space=pltpu.VMEM),
            pl.BlockSpec(memory_space=pl.ANY),
        ],
        out_specs=pl.BlockSpec(memory_space=pltpu.VMEM),
        scratch_shapes=[
            pltpu.VMEM((levels - 1, sn_dev, slots, B * B), jnp.bfloat16),
            pltpu.VMEM((sn_dev, B, slots * B), jnp.bfloat16),
            pltpu.VMEM((slots, B // 2, LANES), jnp.float32),
            pltpu.VMEM(((levels - 1) * sn_lev + 1, B, LANES), jnp.bfloat16),
            pltpu.VMEM((col_count, rows, LANES), jnp.bfloat16),
            pltpu.VMEM((rows, LANES), jnp.float32),
            pltpu.VMEM((rows, LANES), jnp.bfloat16),
            pltpu.VMEM((levels - 1, col_count, rows, LANES), jnp.bfloat16),
            pltpu.VMEM((levels - 1, Z, A, A, 2, rows, LANES), jnp.bfloat16),
            pltpu.VMEM((col_count, rows, LANES), jnp.bfloat16),
            dma((levels - 1,)),
            dma((col_count,)),
            dma((levels - 1, col_count)),
            dma((Z,)),
            dma((Z, A, A)),
            dma((Z, A, A)),
            dma((levels - 1, Z)),
            dma((levels - 1, Z, A, A)),
            dma((levels - 1, Z, A, A)),
            dma((col_count,)),
            dma((col_count,)),
        ],
        compiler_params=pltpu.CompilerParams(
            collective_id=0, has_side_effects=True, vmem_limit_bytes=60 * 1024 * 1024
        ),
    )(pattern, right, inverse, factor)
    return solved.reshape(levels, sn_dev, B * R)


def solution(mesh):
    return jax.shard_map(
        per_device,
        mesh=mesh,
        in_specs=(
            P(None, "row", None),
            P(None, "row", "col", None),
            P(None, "row", None),
            P(None, "row", "col"),
        ),
        out_specs=P(None, "row", None),
        check_vma=False,
    )
```

```python
import functools

import jax
import jax.numpy as jnp
from jax import lax
from jax.experimental import pallas as pl
from jax.experimental.pallas import tpu as pltpu
from jax.sharding import PartitionSpec as P

B = 64
R = 96
LANES = 128
PACK = 48
MESH = pl.DeviceIdType.MESH


def pack(value):
    tail = value[PACK:, :R]
    third = B - PACK
    side = jnp.concatenate([tail[:, 32 * j : 32 * j + 32] for j in range(PACK // third)], axis=0)
    return jnp.concatenate([value[:PACK, :R], side], axis=1)


def unpack_tail(packed):
    third = B - PACK
    parts = [packed[third * j : third * (j + 1), R:] for j in range(PACK // third)]
    return jnp.concatenate(parts, axis=1)


def kernel(
    sizes, pattern_ref, right_ref, inverse_ref, factor_ref, out_ref,
    raw, ready, turn, panels, psend, keep, wide, mine, precv, land, last,
    fsem, red_send, red_recv, z_send, s_send, c_send,
    z_recv, s_recv, c_recv, l_send, l_recv,
):
    levels, sn_dev, slots, Z, A = sizes
    col_count = 2 * A
    row_count = Z * A
    own = sn_dev // col_count
    sn_lev = sn_dev * row_count
    empty = (levels - 1) * sn_lev
    row = lax.axis_index("row")
    col = lax.axis_index("col")
    z, y = row // A, row % A
    x, core = col // 2, col % 2

    def load(level):
        return pltpu.make_async_copy(factor_ref.at[level], raw.at[level - 1], fsem.at[level - 1])

    for level in range(1, levels):
        load(level).start()

    turns = 1 + (z // (Z // 2)) * (Z - 2)
    cols = [(col + d) % col_count for d in range(1, col_count)]

    def plane(d):
        return (z + turns * d) % Z

    def at(r, c):
        return {"row": r, "col": c}

    barrier = pltpu.get_barrier_semaphore()
    for d in range(1, Z):
        pl.semaphore_signal(barrier, inc=1, device_id=at(plane(d) * A + y, col), device_id_type=MESH)
    plane_peers = [
        ((y + d // A) % A, (x + d % A) % A) for d in range(1, A * A)
    ]
    for yt, xt in plane_peers:
        pl.semaphore_signal(barrier, inc=1, device_id=at(z * A + yt, xt * 2 + core), device_id_type=MESH)
    for t in range(A):
        pl.semaphore_signal(barrier, inc=1, device_id=at(row, t * 2 + 1 - core), device_id_type=MESH)

    def remote(src, dst, send, recv, device):
        return pltpu.make_async_remote_copy(
            src_ref=src, dst_ref=dst, send_sem=send, recv_sem=recv,
            device_id=device, device_id_type=MESH,
        )

    def solve(level, summed):
        for u in range(own):
            value = right_ref[level, u]
            if summed is not None:
                value = value - summed[u]
            solved = jnp.dot(
                inverse_ref[level, u], value.astype(jnp.bfloat16), preferred_element_type=jnp.float32
            )
            mine[u * PACK : (u + 1) * PACK, :] = pack(solved).astype(jnp.bfloat16)

    def prepare(level, begin, count):
        low = lax.broadcasted_iota(jnp.int32, (B // 2, LANES), 1) < B

        def body(i, carry):
            for a in range(B // 2):
                turn[:, a, :] = raw[level - 1, i, :, a * LANES : (a + 1) * LANES].astype(jnp.float32)
            for q in range(slots // 2):
                even, odd = turn[2 * q], turn[2 * q + 1]
                lanes = slice(q * LANES, (q + 1) * LANES)
                ready[i, : B // 2, lanes] = jnp.where(low, even, pltpu.roll(odd, B, 1)).astype(jnp.bfloat16)
                ready[i, B // 2 :, lanes] = jnp.where(low, pltpu.roll(even, B, 1), odd).astype(jnp.bfloat16)
            return carry

        lax.fori_loop(begin, begin + count, body, 0)

    def products(level, sent):
        def product(i):
            total = jnp.zeros((B, LANES), jnp.float32)
            for q in range(slots // 4):
                picked = []
                for k in range(4 * q, 4 * q + 4):
                    source = pattern_ref[level, i, k]
                    picked.append(panels[jnp.where(source < 0, empty, source)])
                total += jnp.dot(
                    ready[i, :, 4 * B * q : 4 * B * (q + 1)],
                    jnp.concatenate(picked, axis=0),
                    preferred_element_type=jnp.float32,
                )
            return pack(total)

        def copy(t, source):
            return remote(
                psend.at[t], precv.at[level - 1, source],
                red_send.at[t], red_recv.at[level - 1, source], at(row, t),
            )

        for t in cols:
            def outward(u, carry):
                psend[t, pl.ds(pl.multiple_of(u * PACK, PACK), PACK), :] = product(t * own + u)
                return carry

            lax.fori_loop(0, own, outward, 0)
            copy(t, col).start()

        def inward(u, carry):
            keep[pl.ds(pl.multiple_of(u * PACK, PACK), PACK), :] = product(col * own + u)
            return carry

        lax.fori_loop(0, own, inward, 0)
        sent()
        summed = keep[...]
        for t in cols:
            copy(t, t).wait_recv()
            summed += precv[level - 1, t]
        for t in cols:
            copy(t, col).wait_send()
        values = []
        for u in range(own):
            packed = summed[u * PACK : (u + 1) * PACK]
            split = jnp.concatenate([packed[:, :R], unpack_tail(packed)], axis=0)
            split = jnp.concatenate([split, jnp.zeros((B, LANES - R), jnp.float32)], axis=1)
            for p in range(2):
                wide[u, pl.ds(p, B // 2, stride=2), :] = split[p * (B // 2) : (p + 1) * (B // 2)]
            values.append(wide[u, :, :R])
        return values

    def unpack(level, zc, yc, xc, c):
        base = level * sn_lev + (((zc * A + yc) * A + xc) * 2 + c) * own
        for u in range(own):
            packed = land[level, zc, yc, xc, c, u * PACK : (u + 1) * PACK, :]
            panels[base + u, :PACK, :] = packed
            panels[base + u, PACK:, :R] = unpack_tail(packed)

    def gather(level):
        def z_copy(t, source):
            part = land.at[level, source, y, x, core]
            return remote(part, part, z_send.at[t], z_recv.at[level, source], at(t * A + y, col))

        def p_copy(zc, yt, xt, yc, xc):
            part = land.at[level, zc, yc, xc, core]
            return remote(
                part, part, s_send.at[zc, yt, xt], s_recv.at[level, zc, yc, xc],
                at(z * A + yt, xt * 2 + core),
            )

        def c_copy(zc, yc, xc, c):
            part = land.at[level, zc, yc, xc, c]
            return remote(
                part, part, c_send.at[zc, yc, xc], c_recv.at[level, zc, yc, xc],
                at(row, x * 2 + 1 - core),
            )

        def done(zc, yc, xc):
            c_copy(zc, yc, xc, core).start()
            unpack(level, zc, yc, xc, core)

        def chunk(zc):
            for yt, xt in plane_peers:
                p_copy(zc, yt, xt, y, x).start()
            done(zc, y, x)

        def tail(zc):
            for yt, xt in plane_peers:
                p_copy(zc, yt, xt, yt, xt).wait_recv()
                done(zc, yt, xt)

        land[level, z, y, x, core] = mine[...]
        for d in range(1, Z):
            z_copy(plane(d), z).start()
        chunk(z)
        load(level + 1).wait()
        share = sn_dev // Z
        prepare(level + 1, 0, share)

        def body(d, carry):
            zc = plane(d)
            z_copy(zc, zc).wait_recv()
            chunk(zc)
            prepare(level + 1, d * share, share)
            tail(plane(d - 1))
            return carry

        lax.fori_loop(1, Z, body, 0)
        tail(plane(Z - 1))

        def finish(zc, carry):
            for yc in range(A):
                for xc in range(A):
                    c_copy(zc, yc, xc, 1 - core).wait_recv()
                    unpack(level, zc, yc, xc, 1 - core)
            return carry

        lax.fori_loop(0, Z, finish, 0)

        def settle(zc, carry):
            for yt, xt in plane_peers:
                p_copy(zc, yt, xt, y, x).wait_send()
            for yc in range(A):
                for xc in range(A):
                    c_copy(zc, yc, xc, core).wait_send()
            return carry

        def sent():
            for d in range(1, Z):
                z_copy(plane(d), z).wait_send()
            lax.fori_loop(0, Z, settle, 0)

        return sent

    panels[empty] = jnp.zeros((B, LANES), jnp.bfloat16)
    solve(0, None)
    pl.semaphore_wait(barrier, Z - 1 + A * A - 1 + A)

    def step(level, carry):
        sent = gather(level)
        solve(level + 1, products(level + 1, sent))
        return carry

    lax.fori_loop(0, levels - 1, step, 0)

    top = levels - 1

    def top_copy(t, source):
        return remote(mine, last.at[source], l_send.at[t], l_recv.at[source], at(row, t))

    for t in cols:
        top_copy(t, col).start()
    for level in range(top):
        for i in range(sn_dev):
            out_ref[level, i] = panels[level * sn_lev + row * sn_dev + i, :, :R]
    last[col] = mine[...]
    for t in cols:
        top_copy(t, t).wait_recv()
    for t in cols:
        top_copy(t, col).wait_send()
    for c in range(col_count):
        for u in range(own):
            packed = last[c, u * PACK : (u + 1) * PACK, :]
            out_ref[top, c * own + u, :PACK, :] = packed[:, :R]
            out_ref[top, c * own + u, PACK:, :] = unpack_tail(packed)


def per_device(right_side, factor, diagonal_block_inverse, pattern):
    levels, sn_dev, _ = right_side.shape
    slots = factor.shape[2]
    row_count = lax.axis_size("row")
    col_count = lax.axis_size("col")
    A = col_count // 2
    Z = row_count // A
    own = sn_dev // col_count
    sn_lev = sn_dev * row_count
    first = lax.axis_index("col") * own
    right = lax.dynamic_slice_in_dim(right_side, first, own, 1)
    right = right.reshape(levels, own, B, R)
    inverse = lax.dynamic_slice_in_dim(diagonal_block_inverse, first, own, 1)
    inverse = inverse.reshape(levels, own, B, B)
    dma = pltpu.SemaphoreType.DMA
    rows = own * PACK
    solved = pl.pallas_call(
        functools.partial(kernel, (levels, sn_dev, slots, Z, A)),
        out_shape=jax.ShapeDtypeStruct((levels, sn_dev, B, R), jnp.bfloat16),
        in_specs=[
            pl.BlockSpec(memory_space=pltpu.SMEM),
            pl.BlockSpec(memory_space=pltpu.VMEM),
            pl.BlockSpec(memory_space=pltpu.VMEM),
            pl.BlockSpec(memory_space=pl.ANY),
        ],
        out_specs=pl.BlockSpec(memory_space=pltpu.VMEM),
        scratch_shapes=[
            pltpu.VMEM((levels - 1, sn_dev, slots, B * B), jnp.bfloat16),
            pltpu.VMEM((sn_dev, B, slots * B), jnp.bfloat16),
            pltpu.VMEM((slots, B // 2, LANES), jnp.float32),
            pltpu.VMEM(((levels - 1) * sn_lev + 1, B, LANES), jnp.bfloat16),
            pltpu.VMEM((col_count, rows, LANES), jnp.float32),
            pltpu.VMEM((rows, LANES), jnp.float32),
            pltpu.VMEM((own, B, LANES), jnp.float32),
            pltpu.VMEM((rows, LANES), jnp.bfloat16),
            pltpu.VMEM((levels - 1, col_count, rows, LANES), jnp.float32),
            pltpu.VMEM((levels - 1, Z, A, A, 2, rows, LANES), jnp.bfloat16),
            pltpu.VMEM((col_count, rows, LANES), jnp.bfloat16),
            dma((levels - 1,)),
            dma((col_count,)),
            dma((levels - 1, col_count)),
            dma((Z,)),
            dma((Z, A, A)),
            dma((Z, A, A)),
            dma((levels - 1, Z)),
            dma((levels - 1, Z, A, A)),
            dma((levels - 1, Z, A, A)),
            dma((col_count,)),
            dma((col_count,)),
        ],
        compiler_params=pltpu.CompilerParams(
            collective_id=0, has_side_effects=True, vmem_limit_bytes=60 * 1024 * 1024
        ),
    )(pattern, right, inverse, factor)
    return solved.reshape(levels, sn_dev, B * R)


def solution(mesh):
    return jax.shard_map(
        per_device,
        mesh=mesh,
        in_specs=(
            P(None, "row", None),
            P(None, "row", "col", None),
            P(None, "row", None),
            P(None, "row", "col"),
        ),
        out_specs=P(None, "row", None),
        check_vma=False,
    )
```
